32 devices in a mesh: layer: 4 (over x, core), feat: 2 (over y), width: 4 (over z).
Axes of the slice: x: 2, y: 2, z: 4, core: 2. Of those that a mesh axis runs over, the one named last changes fastest.
Arguments:
- residuals: bfloat16 [4, 64, 2304], P('layer', 'feat', 'width'), may hold values from -6 to 6
- cotangent: bfloat16 [4, 64, 2304], P('layer', 'feat', 'width'), may hold values from -6 to 6
- enc_weight: bfloat16 [4, 2304, 8192], P('layer', 'width', 'feat'), may hold values from -0.125 to 0.125
- enc_bias: float32 [4, 8192], P('layer', 'feat'), may hold values from -3 to 3
- dec_weight: bfloat16 [4, 4, 8192, 2304], P('layer', None, 'feat', 'width'), may hold values from -0.0625 to 0.0625
- active: int32 [4, 64, 8192], P('layer', None, 'feat'), may hold values 0 or 1
Outputs:
- dec_grad: bfloat16 [4, 4, 8192, 2304], P('layer', None, 'feat', 'width')
- enc_grad: bfloat16 [4, 2304, 8192], P('layer', 'width', 'feat')
- bias_grad: float32 [4, 8192], P('layer', 'feat')
- feat_grad: bfloat16 [4, 64, 8192], P('layer', None, 'feat')
The draws below stay inside these ranges and needn't reach their ends.
All inputs are finite; a program needn't handle non-finite values. No bound on the sum of `active` on one device may be relied on, other than what follows from the above.
Results may differ from the reference program's by a relative error of at most 0.005.
Values may be sent and summed in bfloat16 or wider, within the bound.
No kernel may reach another device: no remote copies, remote signals or barrier semaphores. Data moves between devices by JAX's collectives and lax.ppermute only.
A program may use at most 128 MiB of HBM per device.

```python
import jax
import jax.numpy as jnp
from jax import lax

D = 2304
FEAT = 8192
LAYERS = 4
TOKENS = 64


def set_ends(drawn, rng, smallest, largest):
    longest = drawn.shape.index(max(drawn.shape))
    spots = []
    for shift in (0, 1):
        where = [jax.random.randint(jax.random.fold_in(rng, axis), (), 0, length) for axis, length in enumerate(drawn.shape)]
        where[longest] = (where[longest] + shift) % drawn.shape[longest]
        spots.append(tuple(where))
    return drawn.at[spots[0]].set(smallest).at[spots[1]].set(largest)


def steps_of(own_key, dims, cuts, smallest, top_value):
    def one(dim, parts):
        heights = jax.random.uniform(jax.random.fold_in(jax.random.fold_in(own_key, 6), dim), (parts,), jnp.float32, smallest / len(cuts), top_value / len(cuts))
        return jnp.repeat(jnp.exp(heights), dims[dim] // parts).reshape((-1,) + (1,) * (len(dims) - dim - 1))

    gain = one(*cuts[0])
    for cut in cuts[1:]:
        gain = gain * one(*cut)
    return gain


def gaussian(key, extent, scale, most, shards=(), dtype=jnp.bfloat16):
    entries = jax.random.normal(key, extent, jnp.float32) * scale
    if len(shards) > 0:
        entries = steps_of(key, extent, shards, -0.22, 0.18) * entries
    return jnp.clip(entries, min=-most, max=most).astype(dtype)


def setup_inputs(seed: int = 0) -> dict:
    key_list = jax.random.split(jax.random.key(seed), 7)
    residuals = gaussian(key_list[0], (LAYERS, TOKENS, D), 1.0, 6.0, ((0, 4), (1, 2), (2, 4)))
    cotangent = gaussian(key_list[1], (LAYERS, TOKENS, D), 1.0, 6.0, ((0, 4), (1, 2), (2, 4)))
    enc_weight = gaussian(key_list[2], (LAYERS, D, FEAT), D ** -0.5, 0.125, ((0, 4), (1, 4), (2, 2)))
    enc_bias = gaussian(key_list[3], (LAYERS, FEAT), 0.5, 3.0, ((0, 4), (1, 2)), jnp.float32)
    dec_weight = gaussian(key_list[4], (LAYERS, LAYERS, FEAT, D), FEAT ** -0.5, 0.0625, ((0, 4), (2, 2), (3, 4)))
    active = set_ends((jax.random.randint(key_list[5], (LAYERS, TOKENS, FEAT), 0, 2) < 1).astype(jnp.int32), jax.random.fold_in(key_list[5], 1), 0, 1)
    return {"residuals": residuals, "cotangent": cotangent, "enc_weight": enc_weight, "enc_bias": enc_bias, "dec_weight": dec_weight, "active": active}


def reference(residuals, cotangent, enc_weight, enc_bias, dec_weight, active):
    layers = residuals.shape[0]
    dec_rows = []
    enc_rows = []
    bias_rows = []
    feat_rows = []
    for source in range(layers):
        gate_all = active[source].astype(jnp.float32)
        pre_act = jnp.dot(residuals[source], enc_weight[source], preferred_element_type=jnp.float32) + enc_bias[source]
        activation = (pre_act * gate_all).astype(jnp.bfloat16)
        act_grad = jnp.zeros(gate_all.shape, jnp.float32)
        blocks = []
        for target in range(layers):
            if target < source:
                blocks.append(jnp.zeros(dec_weight.shape[2:], jnp.bfloat16))
            else:
                outer = lax.dot_general(activation, cotangent[target], (((0,), (0,)), ((), ())), preferred_element_type=jnp.float32)
                blocks.append(outer.astype(jnp.bfloat16))
                act_grad = act_grad + lax.dot_general(cotangent[target], dec_weight[source, target], (((1,), (1,)), ((), ())), preferred_element_type=jnp.float32)
        feat_grad = (act_grad * gate_all).astype(jnp.bfloat16)
        enc_grad = lax.dot_general(residuals[source], feat_grad, (((0,), (0,)), ((), ())), preferred_element_type=jnp.float32)
        dec_rows.append(jnp.stack(blocks))
        enc_rows.append(enc_grad.astype(jnp.bfloat16))
        bias_rows.append(jnp.sum(feat_grad.astype(jnp.float32), axis=0))
        feat_rows.append(feat_grad)
    return (jnp.stack(dec_rows), jnp.stack(enc_rows), jnp.stack(bias_rows), jnp.stack(feat_rows))
```

```python
import functools

import jax
import jax.numpy as jnp
from jax import lax
from jax.experimental import pallas as pl
from jax.experimental.pallas import tpu as pltpu
from jax.sharding import PartitionSpec as P

MIB = 1 << 20


def tile(extent, most):
    best = extent
    for size in range(128, min(extent, most) + 1, 128):
        if extent % size == 0:
            best = size
    return best


def swap(x, axis, size, bit):
    return lax.ppermute(x, axis, [(i, i ^ bit) for i in range(size)])


def partial_kernel(x_ref, w_ref, keep_ref, send_ref):
    kept = keep_ref.shape[0]
    out = jnp.dot(x_ref[...], w_ref[...], preferred_element_type=jnp.float32)
    keep_ref[...] = out[:kept]
    send_ref[...] = out[kept:].astype(send_ref.dtype)


def partial_product(x, weight, first, count, most):
    rows, depth = x.shape
    half = rows // 2
    width = tile(count, most)
    start = first // width
    return pl.pallas_call(
        partial_kernel,
        grid=(count // width,),
        in_specs=[
            pl.BlockSpec((rows, depth), lambda j: (0, 0)),
            pl.BlockSpec((depth, width), lambda j: (0, start + j)),
        ],
        out_specs=[
            pl.BlockSpec((half, width), lambda j: (0, j)),
            pl.BlockSpec((half, width), lambda j: (0, j)),
        ],
        out_shape=[
            jax.ShapeDtypeStruct((half, count), jnp.float32),
            jax.ShapeDtypeStruct((half, count), jnp.bfloat16),
        ],
        compiler_params=pltpu.CompilerParams(vmem_limit_bytes=40 * MIB),
        cost_estimate=pl.CostEstimate(
            flops=2 * rows * depth * count, bytes_accessed=2 * depth * count, transcendentals=0
        ),
    )(x, weight)


def dec_kernel(pieces, *refs):
    cot_ref, act_refs, out_ref = refs[0], refs[1 : 1 + pieces], refs[1 + pieces]
    act = jnp.concatenate([ref[...] for ref in act_refs], axis=0)
    out_ref[...] = jnp.dot(cot_ref[...], act, preferred_element_type=jnp.float32).astype(out_ref.dtype)


def dec_product(cot_t, acts, most):
    layers, depth, tokens = cot_t.shape
    feats = acts[0].shape[1]
    width = tile(feats, most)
    return pl.pallas_call(
        functools.partial(dec_kernel, len(acts)),
        grid=(feats // width, layers),
        in_specs=[pl.BlockSpec((None, depth, tokens), lambda j, k: (k, 0, 0))]
        + [pl.BlockSpec((a.shape[0], width), lambda j, k: (0, j)) for a in acts],
        out_specs=pl.BlockSpec((None, depth, width), lambda j, k: (k, 0, j)),
        out_shape=jax.ShapeDtypeStruct((layers, depth, feats), jnp.bfloat16),
        compiler_params=pltpu.CompilerParams(vmem_limit_bytes=40 * MIB),
        cost_estimate=pl.CostEstimate(
            flops=2 * layers * tokens * depth * feats,
            bytes_accessed=2 * layers * depth * feats,
            transcendentals=0,
        ),
    )(cot_t, *acts)


def enc_kernel(chained, role_ref, *refs):
    res_ref, mine_ref, other_ref = refs[:3]
    enc_ref, bias_ref, feat_ref = refs[3 + 3 * chained :]
    half = mine_ref.shape[0]
    mine, other = mine_ref[...], other_ref[...]
    grad = jnp.concatenate([mine, other], axis=0)
    enc_ref[...] = jnp.dot(res_ref[...], grad, preferred_element_type=jnp.float32).astype(enc_ref.dtype)
    bias_ref[...] = jnp.sum(grad.astype(jnp.float32), axis=0, keepdims=True)

    @pl.when(role_ref[0] == 0)
    def _():
        feat_ref[:half] = mine
        feat_ref[half:] = other

    @pl.when(role_ref[0] != 0)
    def _():
        feat_ref[:half] = other
        feat_ref[half:] = mine


def enc_product(role, res_t, mine, other, first, feats, before, most):
    depth, tokens = res_t.shape
    half, count = mine.shape
    width = tile(count, most)
    start = first // width
    chained = before is not None
    shapes = [
        jax.ShapeDtypeStruct((depth, feats), jnp.bfloat16),
        jax.ShapeDtypeStruct((1, feats), jnp.float32),
        jax.ShapeDtypeStruct((tokens, feats), jnp.bfloat16),
    ]
    return pl.pallas_call(
        functools.partial(enc_kernel, int(chained)),
        grid_spec=pltpu.PrefetchScalarGridSpec(
            num_scalar_prefetch=1,
            grid=(count // width,),
            in_specs=[
                pl.BlockSpec((depth, tokens), lambda j, r: (0, 0)),
                pl.BlockSpec((half, width), lambda j, r: (0, j)),
                pl.BlockSpec((half, width), lambda j, r: (0, j)),
            ]
            + [pl.BlockSpec(memory_space=pl.ANY)] * (3 * chained),
            out_specs=[
                pl.BlockSpec((depth, width), lambda j, r: (0, start + j)),
                pl.BlockSpec((1, width), lambda j, r: (0, start + j)),
                pl.BlockSpec((tokens, width), lambda j, r: (0, start + j)),
            ],
        ),
        out_shape=shapes,
        input_output_aliases={4: 0, 5: 1, 6: 2} if chained else {},
        compiler_params=pltpu.CompilerParams(vmem_limit_bytes=40 * MIB),
        cost_estimate=pl.CostEstimate(
            flops=2 * tokens * depth * count, bytes_accessed=2 * depth * count, transcendentals=0
        ),
    )(role, res_t, mine, other, *(before if chained else ()))


def both(x, role):
    half = x.shape[-2] // 2
    low, high = x[..., :half, :], x[..., half:, :]
    first = role == 0
    return jnp.concatenate([jnp.where(first, low, high), jnp.where(first, high, low)], axis=-2)


def cross_sum(keep, send, axis, size):
    total = keep + swap(send, axis, size, 1).astype(jnp.float32)
    bit = 2
    while bit < size:
        total = lax.reduce_precision(total, 8, 7)
        total = total + swap(total.astype(jnp.bfloat16), axis, size, bit).astype(jnp.float32)
        bit *= 2
    return total


def rows_of(x, role, half):
    return lax.dynamic_slice_in_dim(x, role * half, half, 0)


def local(feat_size, layer_size, width_size, residuals, cotangent, enc_weight, enc_bias, dec_weight, active):
    layers = dec_weight.shape[1]
    source = lax.axis_index("layer")
    role = lax.axis_index("width") % 2
    role_ref = jnp.reshape(role, (1,)).astype(jnp.int32)
    res, cot = residuals[0], cotangent[0]
    own, depth = res.shape
    feats = enc_weight.shape[2]
    gate = active[0]
    tokens = gate.shape[0]
    weight = jnp.swapaxes(dec_weight[0], 1, 2).reshape(layers * depth, feats)

    if feat_size == 2:
        place = lax.axis_index("feat")
        other = swap(jnp.concatenate([res, cot], axis=0), "feat", 2, 1)
        res_blocks = [res, other[:own]]
        block_rows = [place * own, (1 - place) * own]
        cot_own_first = jnp.concatenate([cot, other[own:]], axis=0)
        res_all = jnp.where(place == 0, jnp.concatenate(res_blocks, 0), jnp.concatenate(res_blocks[::-1], 0))
    else:
        res_all = lax.all_gather(res, "feat", axis=0, tiled=True)
        cot_own_first = lax.all_gather(cot, "feat", axis=0, tiled=True)
        res_blocks = [res_all]
        block_rows = [0]

    acts = []
    for rows, first in zip(res_blocks, block_rows):
        keep, send = partial_product(both(rows, role), enc_weight[0], 0, feats, 512)
        total = cross_sum(keep, send, "width", width_size)
        half = total.shape[0]
        mask = lax.dynamic_slice_in_dim(gate, first + role * half, half, 0).astype(jnp.float32)
        act = ((total + enc_bias) * mask).astype(jnp.bfloat16)
        acts += [act, swap(act, "width", width_size, 1)]

    held = [cot_own_first]
    bit = layer_size // 2
    while bit:
        held = held + list(swap(jnp.stack(held), "layer", layer_size, bit))
        bit //= 2
    order = [0]
    bit = layer_size // 2
    while bit:
        order = order + [o ^ bit for o in order]
        bit //= 2
    by_xor = [held[order.index(j)] for j in range(layer_size)]
    grads = jnp.stack(by_xor)
    grads = jnp.take(grads, jnp.arange(layers) ^ source, axis=0)
    later = (jnp.arange(layers) >= source)[:, None, None]
    grads = jnp.where(later, grads, jnp.zeros_like(grads))
    if feat_size == 2:
        grads_true = jnp.where(place == 0, grads, jnp.roll(grads, own, axis=1))
    else:
        grads_true = grads
    rows_true = both(grads_true, role)
    lhs = jnp.swapaxes(rows_true, 0, 1).reshape(tokens, layers * depth)

    parts = 2
    count = feats // parts
    half = tokens // 2
    mask = rows_of(gate, role, half).astype(jnp.float32)
    mine, theirs = [], []
    for part in range(parts):
        keep, send = partial_product(lhs, weight, part * count, count, 512)
        total = cross_sum(keep, send, "width", width_size)
        grad = (total * mask[:, part * count : (part + 1) * count]).astype(jnp.bfloat16)
        mine.append(grad)
        theirs.append(swap(grad, "width", width_size, 1))

    ends = [sum(r.shape[0] for r in res_blocks[:i]) for i in range(len(res_blocks) + 1)]
    rows_act = jnp.concatenate([both(grads[:, a:b], role) for a, b in zip(ends, ends[1:])], axis=1)
    dec_grad = dec_product(jnp.swapaxes(rows_act, 1, 2), acts, 1024)

    res_t = both(res_all, role).T
    out = None
    for part in range(parts):
        out = enc_product(role_ref, res_t, mine[part], theirs[part], part * count, feats, out, 512)
    enc_grad, bias_grad, feat_grad = out
    return (jnp.swapaxes(dec_grad, 1, 2)[None], enc_grad[None], bias_grad, feat_grad[None])


def solution(mesh):
    in_specs = (
        P("layer", "feat", "width"),
        P("layer", "feat", "width"),
        P("layer", "width", "feat"),
        P("layer", "feat"),
        P("layer", None, "feat", "width"),
        P("layer", None, "feat"),
    )
    out_specs = (
        P("layer", None, "feat", "width"),
        P("layer", "width", "feat"),
        P("layer", "feat"),
        P("layer", None, "feat"),
    )
    sizes = (mesh.shape["feat"], mesh.shape["layer"], mesh.shape["width"])
    return jax.shard_map(
        functools.partial(local, *sizes), mesh=mesh, in_specs=in_specs, out_specs=out_specs, check_vma=False
    )
```

```python
import functools

import jax
import jax.numpy as jnp
from jax import lax
from jax.experimental import pallas as pl
from jax.experimental.pallas import tpu as pltpu
from jax.sharding import PartitionSpec as P

MIB = 1 << 20
VMEM = pl.BlockSpec(memory_space=pltpu.VMEM)
SMEM = pl.BlockSpec(memory_space=pltpu.SMEM)
ANY = pl.BlockSpec(memory_space=pl.ANY)
HBM = pl.BlockSpec(memory_space=pltpu.HBM)
LIMIT = 16 * MIB
FEAT_LIMIT = 16 * MIB
JA2 = False
JB2 = False
KBW = False
DEC_LIMIT = 24 * MIB
JOINT = False
EPARTS = 1
DPARTS = 2
ORDER = {
    "feat": lambda part, sums, ready: () if part == 0 else (sums[0],),
    "dec": lambda part, sums, ready: (sums[0],) if part == 0 else (ready[0],),
}


def tile(extent, most):
    best = extent
    for size in range(128, min(extent, most) + 1, 128):
        if extent % size == 0:
            best = size
    return best


def swap(x, axis, size, bit):
    return lax.ppermute(x, axis, [(i, i ^ bit) for i in range(size)])


def cost(rows, depth, columns, passed):
    return pl.CostEstimate(flops=2 * rows * depth * columns, bytes_accessed=passed, transcendentals=0)


def in_hbm(x):
    return pltpu.with_memory_space_constraint(x, pltpu.HBM)


def ordered(low, first, second):
    return jnp.concatenate([jnp.where(low, first, second), jnp.where(low, second, first)], axis=0)


def enc_part_kernel(steps, role_ref, x_ref, w_hbm, *refs):
    keep_ref, send_ref, w_ref, x_buf, acc, x_sem, sems = refs[-7:]
    half = keep_ref.shape[0]
    rows = w_ref.shape[0] // steps

    def get(i):
        here = pl.ds(i * rows, rows)
        return pltpu.make_async_copy(w_hbm.at[here], w_ref.at[here], sems.at[i])

    x_copy = pltpu.make_async_copy(x_ref, x_buf, x_sem)
    x_copy.start()
    for i in range(steps):
        get(i).start()
    x_copy.wait()
    x = ordered(role_ref[0] == 0, x_buf[:half], x_buf[half:])
    for i in range(steps):
        get(i).wait()
        here = slice(i * rows, (i + 1) * rows)
        out = jnp.dot(x[:, here], w_ref[here], preferred_element_type=jnp.float32)
        if i:
            out += acc[...]
        if i < steps - 1:
            acc[...] = out
        else:
            keep_ref[...] = out[:half]
            send_ref[...] = out[half:].astype(send_ref.dtype)


def enc_part(role, x, weight, after=()):
    rows, depth = x.shape
    feats = weight.shape[1]
    half = rows // 2
    steps = next(n for n in (9, 8, 4, 2, 1) if depth % (16 * n) == 0)
    return pl.pallas_call(
        functools.partial(enc_part_kernel, steps),
        in_specs=[SMEM, ANY, HBM] + [ANY] * len(after),
        out_specs=[VMEM, VMEM],
        out_shape=[
            jax.ShapeDtypeStruct((half, feats), jnp.float32),
            jax.ShapeDtypeStruct((half, feats), jnp.bfloat16),
        ],
        scratch_shapes=[
            pltpu.VMEM((depth, feats), jnp.bfloat16),
            pltpu.VMEM((rows, depth), jnp.bfloat16),
            pltpu.VMEM((rows, feats), jnp.float32),
            pltpu.SemaphoreType.DMA,
            pltpu.SemaphoreType.DMA((steps,)),
        ],
        compiler_params=pltpu.CompilerParams(vmem_limit_bytes=LIMIT),
        cost_estimate=cost(rows, depth, feats, 2 * depth * feats),
    )(role, x, in_hbm(weight), *after)


def feat_part_kernel(first, pieces, ids_ref, *refs):
    piece_refs, w_hbm = refs[:pieces], refs[pieces]
    keep_ref, send_ref, w_buf, acc, sems = refs[-5:]
    half, count = keep_ref.shape
    source = ids_ref[0]

    def get(k):
        return pltpu.make_async_copy(w_hbm.at[source ^ k, :, pl.ds(first, count)], w_buf.at[k], sems.at[k])

    for k in range(pieces):
        get(k).start()
    for k in range(pieces):
        rows = piece_refs[k][...]
        rows = jnp.where((source ^ k) >= source, rows, jnp.zeros_like(rows))
        rows = ordered(ids_ref[1] == 0, rows[:half], rows[half:])
        get(k).wait()
        out = jnp.dot(rows, w_buf[k], preferred_element_type=jnp.float32)
        if k:
            out += acc[...]
        if k < pieces - 1:
            acc[...] = out
        else:
            keep_ref[...] = out[:half]
            send_ref[...] = out[half:].astype(send_ref.dtype)


def feat_part(ids, grads, weight, first, count, after=()):
    tokens, depth = grads[0].shape
    half = tokens // 2
    return pl.pallas_call(
        functools.partial(feat_part_kernel, first, len(grads)),
        in_specs=[SMEM] + [VMEM] * len(grads) + [HBM] + [ANY] * len(after),
        out_specs=[VMEM, VMEM],
        out_shape=[
            jax.ShapeDtypeStruct((half, count), jnp.float32),
            jax.ShapeDtypeStruct((half, count), jnp.bfloat16),
        ],
        scratch_shapes=[
            pltpu.VMEM((len(grads), depth, count), jnp.bfloat16),
            pltpu.VMEM((tokens, count), jnp.float32),
            pltpu.SemaphoreType.DMA((len(grads),)),
        ],
        compiler_params=pltpu.CompilerParams(vmem_limit_bytes=FEAT_LIMIT),
        cost_estimate=cost(tokens, len(grads) * depth, count, 2 * len(grads) * depth * count),
    )(ids, *grads, in_hbm(weight), *after)


def dec_kernel(first_block, blocks, width, kept, ids_ref, grad_refs, act_refs, out_hbm, act_buf, out_buf, sems):
    source = ids_ref[0]
    first = ids_ref[2] == 0
    start = 0
    for mine_ref, other_ref in zip(act_refs[::2], act_refs[1::2]):
        for row in range(0, mine_ref.shape[0], kept):
            mine, other = mine_ref[row : row + kept], other_ref[row : row + kept]
            act_buf[start : start + kept] = jnp.where(first, mine, other)
            act_buf[start + kept : start + 2 * kept] = jnp.where(first, other, mine)
            start += 2 * kept
    steps = act_buf.shape[1] // width

    def put(b, j):
        columns = pl.ds(j * width, width)
        return pltpu.make_async_copy(
            out_buf.at[b, :, columns], out_hbm.at[source ^ (first_block + b), :, columns], sems.at[b, j]
        )

    for b in range(blocks):
        grad = grad_refs[first_block + b][...]
        grad = jnp.where((source ^ (first_block + b)) >= source, grad, jnp.zeros_like(grad)).T
        for j in range(steps):
            columns = slice(j * width, (j + 1) * width)
            out = jnp.dot(grad, act_buf[:, columns], preferred_element_type=jnp.float32)
            out_buf[b, :, columns] = out.astype(out_buf.dtype)
            put(b, j).start()
    for b in range(blocks):
        for j in range(steps):
            put(b, j).wait()


def dec_product(ids, grads, acts, kept, first, blocks, before=None, after=()):
    tokens, depth = grads[0].shape
    layers = len(grads)
    feats = acts[0].shape[1]
    held = () if before is None else (before,)
    width = tile(feats, 1024)

    def body(ids_ref, *refs):
        dec_kernel(
            first, blocks, width, kept, ids_ref, refs[:layers], refs[layers : layers + len(acts)], refs[-4], *refs[-3:]
        )

    return pl.pallas_call(
        body,
        in_specs=[SMEM] + [VMEM] * (layers + len(acts)) + [ANY] * (len(held) + len(after)),
        out_specs=HBM,
        out_shape=jax.ShapeDtypeStruct((layers, depth, feats), jnp.bfloat16),
        scratch_shapes=[
            pltpu.VMEM((tokens, feats), jnp.bfloat16),
            pltpu.VMEM((blocks, depth, feats), jnp.bfloat16),
            pltpu.SemaphoreType.DMA((blocks, feats // width)),
        ],
        input_output_aliases={1 + layers + len(acts): 0} if held else {},
        compiler_params=pltpu.CompilerParams(vmem_limit_bytes=DEC_LIMIT),
        cost_estimate=cost(blocks * tokens, depth, feats, 2 * blocks * depth * feats),
    )(ids, *grads, *acts, *held, *after)


def enc_kernel(first_column, width, res_refs, ids_ref, mine_ref, other_ref, enc_hbm, bias_hbm, feat_hbm, res_t, enc_buf, bias_buf, feat_buf, sems):
    count = enc_buf.shape[1]
    low, first = ids_ref[1] == 0, ids_ref[2] == 0
    res_t[...] = jnp.concatenate([ref[...] for ref in res_refs], axis=0).T
    mine, other = mine_ref[...], other_ref[...]
    feat_buf[...] = jnp.concatenate([jnp.where(first, mine, other), jnp.where(first, other, mine)], axis=0)
    here = pl.ds(first_column, count)
    puts = [pltpu.make_async_copy(feat_buf, feat_hbm.at[:, here], sems.at[0])]
    puts[0].start()
    grad = jnp.concatenate([jnp.where(low, mine, other), jnp.where(low, other, mine)], axis=0)
    for j in range(count // width):
        columns = slice(j * width, (j + 1) * width)
        out = jnp.dot(res_t[...], grad[:, columns], preferred_element_type=jnp.float32)
        enc_buf[:, columns] = out.astype(enc_buf.dtype)
        puts.append(
            pltpu.make_async_copy(
                enc_buf.at[:, columns], enc_hbm.at[:, pl.ds(first_column + j * width, width)], sems.at[2 + j]
            )
        )
        puts[-1].start()
    bias_buf[...] = jnp.sum(grad.astype(jnp.float32), axis=0, keepdims=True)
    puts.append(pltpu.make_async_copy(bias_buf, bias_hbm.at[:, here], sems.at[1]))
    puts[-1].start()
    for put in puts:
        put.wait()


def enc_product(ids, blocks, mine, other, first, feats, before=None, after=()):
    depth = blocks[0].shape[1]
    half, count = mine.shape
    tokens = 2 * half
    width = tile(count, 512)
    held = () if before is None else tuple(before)
    extra = len(held) + len(after)

    def body(ids_ref, *refs):
        ends = refs[len(blocks) + 2 + extra :]
        enc_kernel(first, width, refs[: len(blocks)], ids_ref, *refs[len(blocks) : len(blocks) + 2], *ends)

    at = 3 + len(blocks)
    return pl.pallas_call(
        body,
        in_specs=[SMEM] + [VMEM] * (len(blocks) + 2) + [ANY] * extra,
        out_specs=[HBM] * 3,
        out_shape=[
            jax.ShapeDtypeStruct((depth, feats), jnp.bfloat16),
            jax.ShapeDtypeStruct((1, feats), jnp.float32),
            jax.ShapeDtypeStruct((tokens, feats), jnp.bfloat16),
        ],
        scratch_shapes=[
            pltpu.VMEM((depth, tokens), jnp.bfloat16),
            pltpu.VMEM((depth, count), jnp.bfloat16),
            pltpu.VMEM((1, count), jnp.float32),
            pltpu.VMEM((tokens, count), jnp.bfloat16),
            pltpu.SemaphoreType.DMA((2 + count // width,)),
        ],
        input_output_aliases={at: 0, at + 1: 1, at + 2: 2} if held else {},
        compiler_params=pltpu.CompilerParams(vmem_limit_bytes=LIMIT),
        cost_estimate=cost(tokens, depth, count, 2 * depth * count),
    )(ids, *blocks, mine, other, *held, *after)


def rounded(x):
    return lax.reduce_precision(x, 8, 7)


def local(feat_size, layer_size, width_size, residuals, cotangent, enc_weight, enc_bias, dec_weight, active):
    layers = dec_weight.shape[1]
    source = lax.axis_index("layer")
    role = lax.axis_index("width") % 2
    res, cot = residuals[0], cotangent[0]
    own, depth = res.shape
    feats = enc_weight.shape[2]
    gate = active[0]
    tokens = gate.shape[0]
    half = tokens // 2
    weight = jnp.swapaxes(dec_weight[0], 1, 2)
    role_ref = jnp.reshape(role, (1,)).astype(jnp.int32)

    def neighbour(x):
        return swap(x, "width", width_size, 1)

    def across(x):
        bit, stage = 2, x
        while bit < width_size:
            x = rounded(x)
            stage = x.astype(jnp.bfloat16)
            x = x + swap(stage, "width", width_size, bit).astype(jnp.float32)
            bit *= 2
        return x, stage

    if feat_size == 2:
        place = lax.axis_index("feat")
        sent = lax.optimization_barrier(jnp.concatenate([res, cot], axis=0))
        other = swap(sent, "feat", 2, 1)
        blocks = [res, other[:own]]
        starts = [place * own, (1 - place) * own]
        grads = jnp.concatenate([sent[own:], other[own:]], axis=0)
    else:
        place = 0
        blocks = [lax.all_gather(res, "feat", axis=0, tiled=True)]
        starts = [0]
        grads = lax.all_gather(cot, "feat", axis=0, tiled=True)
    low = role ^ place
    ids = jnp.stack([source, low, role]).astype(jnp.int32)

    held, order = [grads], [0]
    bit = layer_size // 2
    while bit:
        got = swap(jnp.stack(held), "layer", layer_size, bit)
        held = held + [got[i] for i in range(len(held))]
        order = order + [o ^ bit for o in order]
        bit //= 2
    grads = [held[order.index(j)] for j in range(layer_size)]

    sides, gates, sums, ready, acts = [], [], [], [], []
    after = ()
    for rows, first in zip(blocks, starts):
        keep, send = enc_part(role_ref, in_hbm(rows) if rows is res else rows, enc_weight[0], after)
        after = (send,)
        sides.append(keep + neighbour(send).astype(jnp.float32))
        kept = keep.shape[0]
        gates.append(lax.dynamic_slice_in_dim(gate, first + role * kept, kept, 0).astype(jnp.float32))
    if JOINT:
        sides, gates = [jnp.concatenate(sides, axis=0)], [jnp.concatenate(gates, axis=0)]
    if KBW:
        whole = feat_part(ids, grads, weight, 0, feats, ORDER["feat"](0, sums, ready))
    for pair, mask in zip(sides, gates):
        total, stage = across(pair)
        sums.append(stage)
        act = ((total + enc_bias) * mask).astype(jnp.bfloat16)
        ready.append(act)
        if not JA2:
            acts += [act, neighbour(act)]
    if JA2:
        act = jnp.concatenate(ready, axis=0)
        acts = [act, neighbour(act)]

    parts = 2
    count = feats // parts
    mask = lax.dynamic_slice_in_dim(gate, role * half, half, 0).astype(jnp.float32)
    pairs, feat_sums, feat_ready = [], [], []
    for part in range(parts):
        if KBW:
            keep, send = [w[:, part * count : (part + 1) * count] for w in whole]
        else:
            keep, send = feat_part(ids, grads, weight, part * count, count, ORDER["feat"](part, sums, ready))
        pair = keep + neighbour(send).astype(jnp.float32)
        total, stage = across(pair)
        feat_sums.append(stage)
        grad = (total * mask[:, part * count : (part + 1) * count]).astype(jnp.bfloat16)
        feat_ready.append(grad)
        if not JB2:
            pairs.append((grad, neighbour(grad)))
    if JB2:
        grad = jnp.concatenate(feat_ready, axis=1)
        pairs = [(grad, neighbour(grad))]

    dec_grad = None
    for part in range(DPARTS):
        dec_grad = dec_product(ids, grads, acts, blocks[0].shape[0] // 2, part * layers // DPARTS, layers // DPARTS, dec_grad, ORDER["dec"](part, feat_sums, feat_ready))

    out = None
    if EPARTS == 1 and not JB2:
        pairs = [[jnp.concatenate(side, axis=1) for side in zip(*pairs)]]
    for part in range(EPARTS):
        out = enc_product(ids, blocks, *pairs[part], part * feats // EPARTS, feats, out)
    enc_grad, bias_grad, feat_grad = out
    return (jnp.swapaxes(dec_grad, 1, 2)[None], enc_grad[None], bias_grad, feat_grad[None])


def solution(mesh):
    in_specs = (
        P("layer", "feat", "width"),
        P("layer", "feat", "width"),
        P("layer", "width", "feat"),
        P("layer", "feat"),
        P("layer", None, "feat", "width"),
        P("layer", None, "feat"),
    )
    out_specs = (
        P("layer", None, "feat", "width"),
        P("layer", "width", "feat"),
        P("layer", "feat"),
        P("layer", None, "feat"),
    )
    sizes = (mesh.shape["feat"], mesh.shape["layer"], mesh.shape["width"])
    return jax.shard_map(
        functools.partial(local, *sizes), mesh=mesh, in_specs=in_specs, out_specs=out_specs, check_vma=False
    )
```

```python
import functools

import jax
import jax.numpy as jnp
from jax import lax
from jax.experimental import pallas as pl
from jax.experimental.pallas import tpu as pltpu
from jax.sharding import PartitionSpec as P

MIB = 1 << 20
VMEM = pl.BlockSpec(memory_space=pltpu.VMEM)
ANY = pl.BlockSpec(memory_space=pl.ANY)
HBM = pl.BlockSpec(memory_space=pltpu.HBM)
LIMIT = 16 * MIB
DEC_LIMIT = 24 * MIB


def tile(extent, most):
    best = extent
    for size in range(128, min(extent, most) + 1, 128):
        if extent % size == 0:
            best = size
    return best


def swap(x, axis, size, bit):
    return lax.ppermute(x, axis, [(i, i ^ bit) for i in range(size)])


def cost(rows, depth, columns, passed):
    return pl.CostEstimate(flops=2 * rows * depth * columns, bytes_accessed=passed, transcendentals=0)


def in_hbm(x):
    return pltpu.with_memory_space_constraint(x, pltpu.HBM)


def place_of(feat_size):
    role = lax.rem(lax.axis_index("width"), 2)
    place = lax.axis_index("feat") if feat_size == 2 else 0
    return lax.axis_index("layer"), role ^ place, role


def ordered(low, first, second):
    return jnp.concatenate([jnp.where(low, first, second), jnp.where(low, second, first)], axis=0)


def enc_part_kernel(steps, x_ref, w_hbm, *refs):
    keep_ref, send_ref, w_ref, x_buf, acc, x_sem, sems = refs[-7:]
    half = keep_ref.shape[0]
    rows = w_ref.shape[0] // steps

    def get(i):
        here = pl.ds(i * rows, rows)
        return pltpu.make_async_copy(w_hbm.at[here], w_ref.at[here], sems.at[i])

    x_copy = pltpu.make_async_copy(x_ref, x_buf, x_sem)
    x_copy.start()
    for i in range(steps):
        get(i).start()
    x_copy.wait()
    x = ordered(place_of(0)[2] == 0, x_buf[:half], x_buf[half:])
    for i in range(steps):
        get(i).wait()
        here = slice(i * rows, (i + 1) * rows)
        out = jnp.dot(x[:, here], w_ref[here], preferred_element_type=jnp.float32)
        if i:
            out += acc[...]
        if i < steps - 1:
            acc[...] = out
        else:
            keep_ref[...] = out[:half]
            send_ref[...] = out[half:].astype(send_ref.dtype)


def enc_part(x, weight, after=()):
    rows, depth = x.shape
    feats = weight.shape[1]
    half = rows // 2
    steps = next(n for n in (3, 2, 1) if depth % (16 * n) == 0)
    return pl.pallas_call(
        functools.partial(enc_part_kernel, steps),
        in_specs=[ANY, HBM] + [ANY] * len(after),
        out_specs=[VMEM, VMEM],
        out_shape=[
            jax.ShapeDtypeStruct((half, feats), jnp.float32),
            jax.ShapeDtypeStruct((half, feats), jnp.bfloat16),
        ],
        scratch_shapes=[
            pltpu.VMEM((depth, feats), jnp.bfloat16),
            pltpu.VMEM((rows, depth), jnp.bfloat16),
            pltpu.VMEM((rows, feats), jnp.float32),
            pltpu.SemaphoreType.DMA,
            pltpu.SemaphoreType.DMA((steps,)),
        ],
        compiler_params=pltpu.CompilerParams(vmem_limit_bytes=LIMIT),
        cost_estimate=cost(rows, depth, feats, 2 * depth * feats),
    )(x, in_hbm(weight), *after)


def feat_part_kernel(feat_size, first, pieces, *refs):
    piece_refs, w_hbm = refs[:pieces], refs[pieces]
    keep_ref, send_ref, w_buf, acc, sems = refs[-5:]
    half, count = keep_ref.shape
    source, low, _ = place_of(feat_size)

    def get(k):
        return pltpu.make_async_copy(w_hbm.at[source ^ k, :, pl.ds(first, count)], w_buf.at[k], sems.at[k])

    for k in range(pieces):
        get(k).start()
    for k in range(pieces):
        rows = piece_refs[k][...]
        rows = jnp.where((source ^ k) >= source, rows, jnp.zeros_like(rows))
        rows = ordered(low == 0, rows[:half], rows[half:])
        get(k).wait()
        out = jnp.dot(rows, w_buf[k], preferred_element_type=jnp.float32)
        if k:
            out += acc[...]
        if k < pieces - 1:
            acc[...] = out
        else:
            keep_ref[...] = out[:half]
            send_ref[...] = out[half:].astype(send_ref.dtype)


def feat_part(feat_size, grads, weight, first, count, after=()):
    tokens, depth = grads[0].shape
    half = tokens // 2
    return pl.pallas_call(
        functools.partial(feat_part_kernel, feat_size, first, len(grads)),
        in_specs=[VMEM] * len(grads) + [HBM] + [ANY] * len(after),
        out_specs=[VMEM, VMEM],
        out_shape=[
            jax.ShapeDtypeStruct((half, count), jnp.float32),
            jax.ShapeDtypeStruct((half, count), jnp.bfloat16),
        ],
        scratch_shapes=[
            pltpu.VMEM((len(grads), depth, count), jnp.bfloat16),
            pltpu.VMEM((tokens, count), jnp.float32),
            pltpu.SemaphoreType.DMA((len(grads),)),
        ],
        compiler_params=pltpu.CompilerParams(vmem_limit_bytes=LIMIT),
        cost_estimate=cost(tokens, len(grads) * depth, count, 2 * len(grads) * depth * count),
    )(*grads, in_hbm(weight), *after)


def dec_kernel(first_block, blocks, width, kept, grad_refs, act_refs, out_hbm, act_buf, out_buf, sems):
    source, _, role = place_of(0)
    first = role == 0
    start = 0
    for mine_ref, other_ref in zip(act_refs[::2], act_refs[1::2]):
        for row in range(0, mine_ref.shape[0], kept):
            mine, other = mine_ref[row : row + kept], other_ref[row : row + kept]
            act_buf[start : start + kept] = jnp.where(first, mine, other)
            act_buf[start + kept : start + 2 * kept] = jnp.where(first, other, mine)
            start += 2 * kept
    steps = act_buf.shape[1] // width

    def put(b, j):
        columns = pl.ds(j * width, width)
        return pltpu.make_async_copy(
            out_buf.at[b, :, columns], out_hbm.at[source ^ (first_block + b), :, columns], sems.at[b, j]
        )

    for b in range(blocks):
        grad = grad_refs[first_block + b][...]
        grad = jnp.where((source ^ (first_block + b)) >= source, grad, jnp.zeros_like(grad)).T
        for j in range(steps):
            columns = slice(j * width, (j + 1) * width)
            out = jnp.dot(grad, act_buf[:, columns], preferred_element_type=jnp.float32)
            out_buf[b, :, columns] = out.astype(out_buf.dtype)
            put(b, j).start()
    for b in range(blocks):
        for j in range(steps):
            put(b, j).wait()


def dec_product(grads, acts, kept, first, blocks, before=None, after=()):
    tokens, depth = grads[0].shape
    layers = len(grads)
    feats = acts[0].shape[1]
    held = () if before is None else (before,)
    width = tile(feats, 1024)

    def body(*refs):
        dec_kernel(
            first, blocks, width, kept, refs[:layers], refs[layers : layers + len(acts)], refs[-4], *refs[-3:]
        )

    return pl.pallas_call(
        body,
        in_specs=[VMEM] * (layers + len(acts)) + [ANY] * (len(held) + len(after)),
        out_specs=HBM,
        out_shape=jax.ShapeDtypeStruct((layers, depth, feats), jnp.bfloat16),
        scratch_shapes=[
            pltpu.VMEM((tokens, feats), jnp.bfloat16),
            pltpu.VMEM((blocks, depth, feats), jnp.bfloat16),
            pltpu.SemaphoreType.DMA((blocks, feats // width)),
        ],
        input_output_aliases={layers + len(acts): 0} if held else {},
        compiler_params=pltpu.CompilerParams(vmem_limit_bytes=DEC_LIMIT),
        cost_estimate=cost(blocks * tokens, depth, feats, 2 * blocks * depth * feats),
    )(*grads, *acts, *held, *after)


def enc_kernel(feat_size, width, res_refs, mine_refs, other_refs, outs, res_t, enc_buf, bias_buf, feat_buf, sems):
    enc_hbm, bias_hbm, feat_hbm = outs
    _, low, role = place_of(feat_size)
    low, first = low == 0, role == 0
    res_t[...] = jnp.concatenate([ref[...] for ref in res_refs], axis=0).T
    puts = []

    def put(source, target):
        puts.append(pltpu.make_async_copy(source, target, sems.at[len(puts)]))
        puts[-1].start()

    start = 0
    for mine_ref, other_ref in zip(mine_refs, other_refs):
        count = mine_ref.shape[1]
        here = pl.ds(start, count)
        mine, other = mine_ref[...], other_ref[...]
        feat_buf[:, here] = jnp.concatenate([jnp.where(first, mine, other), jnp.where(first, other, mine)], axis=0)
        put(feat_buf.at[:, here], feat_hbm.at[:, here])
        grad = jnp.concatenate([jnp.where(low, mine, other), jnp.where(low, other, mine)], axis=0)
        for j in range(0, count, width):
            out = jnp.dot(res_t[...], grad[:, j : j + width], preferred_element_type=jnp.float32)
            columns = pl.ds(start + j, width)
            enc_buf[:, columns] = out.astype(enc_buf.dtype)
            put(enc_buf.at[:, columns], enc_hbm.at[:, columns])
        bias_buf[:, here] = jnp.sum(grad.astype(jnp.float32), axis=0, keepdims=True)
        start += count
    put(bias_buf, bias_hbm)
    for copy in puts:
        copy.wait()


def enc_product(feat_size, blocks, mine, others):
    depth = blocks[0].shape[1]
    tokens = 2 * mine[0].shape[0]
    feats = sum(x.shape[1] for x in mine)
    width = tile(mine[0].shape[1], 512)
    ends = [len(blocks), len(blocks) + len(mine), len(blocks) + 2 * len(mine)]

    def body(*refs):
        pieces = refs[: ends[0]], refs[ends[0] : ends[1]], refs[ends[1] : ends[2]]
        enc_kernel(feat_size, width, *pieces, refs[ends[2] : ends[2] + 3], *refs[ends[2] + 3 :])

    return pl.pallas_call(
        body,
        in_specs=[VMEM] * ends[2],
        out_specs=[HBM] * 3,
        out_shape=[
            jax.ShapeDtypeStruct((depth, feats), jnp.bfloat16),
            jax.ShapeDtypeStruct((1, feats), jnp.float32),
            jax.ShapeDtypeStruct((tokens, feats), jnp.bfloat16),
        ],
        scratch_shapes=[
            pltpu.VMEM((depth, tokens), jnp.bfloat16),
            pltpu.VMEM((depth, feats), jnp.bfloat16),
            pltpu.VMEM((1, feats), jnp.float32),
            pltpu.VMEM((tokens, feats), jnp.bfloat16),
            pltpu.SemaphoreType.DMA((1 + len(mine) + feats // width,)),
        ],
        compiler_params=pltpu.CompilerParams(vmem_limit_bytes=LIMIT),
        cost_estimate=cost(tokens, depth, feats, 2 * depth * feats),
    )(*blocks, *mine, *others)


def after(x, *others):
    return lax.optimization_barrier((x, *others))[0] if others else x


def rounded(x):
    return lax.reduce_precision(x, 8, 7)


def local(feat_size, layer_size, width_size, residuals, cotangent, enc_weight, enc_bias, dec_weight, active):
    layers = dec_weight.shape[1]
    source = lax.axis_index("layer")
    role = lax.axis_index("width") % 2
    res, cot = residuals[0], cotangent[0]
    own, depth = res.shape
    feats = enc_weight.shape[2]
    gate = active[0]
    tokens = gate.shape[0]
    weight = jnp.swapaxes(dec_weight[0], 1, 2)

    def neighbour(x):
        return swap(x, "width", width_size, 1)

    def pair_sum(keep, got, *before):
        got = after(got, *before)
        total = rounded(keep + got.astype(jnp.float32))
        return total, total.astype(jnp.bfloat16)

    def across(total, stage):
        bit, parts = 2, []
        while bit < width_size:
            if parts:
                total = rounded(total + parts.pop().astype(jnp.float32))
                stage = total.astype(jnp.bfloat16)
            parts.append(swap(stage, "width", width_size, bit))
            bit *= 2
        return total, parts

    def whole_sum(total, parts, *before):
        for part in parts:
            total = total + after(part, *before).astype(jnp.float32)
        return total

    if feat_size == 2:
        place = lax.axis_index("feat")
        sent = lax.optimization_barrier(jnp.concatenate([res, cot], axis=0))
        halves = [enc_part(in_hbm(res), enc_weight[0])]
        other = after(swap(sent, "feat", 2, 1), halves[0][1])
        blocks = [res, other[:own]]
        starts = [place * own, (1 - place) * own]
        grads = jnp.concatenate([sent[own:], other[own:]], axis=0)
    else:
        place, halves = 0, []
        blocks = [lax.all_gather(res, "feat", axis=0, tiled=True)]
        starts = [0]
        grads = lax.all_gather(cot, "feat", axis=0, tiled=True)
    held, order = [grads], [0]
    bit = layer_size // 2
    while bit:
        got = swap(jnp.stack(held), "layer", layer_size, bit)
        held = held + [got[i] for i in range(len(held))]
        order = order + [o ^ bit for o in order]
        bit //= 2
    grads = [held[order.index(j)] for j in range(layer_size)]

    for rows in blocks[len(halves) :]:
        halves.append(enc_part(rows, enc_weight[0]))
    got = [neighbour(send) for _, send in halves]
    act_sums = []
    for (keep, _), other in zip(halves, got):
        act_sums.append(across(*pair_sum(keep, other, *[total for total, _ in act_sums[-1:]])))

    def activation(i, *before):
        kept = halves[i][0].shape[0]
        mask = lax.dynamic_slice_in_dim(gate, starts[i] + role * kept, kept, 0).astype(jnp.float32)
        return ((whole_sum(*act_sums[i], *before) + enc_bias) * mask).astype(jnp.bfloat16)

    count = feats // 2
    half = tokens // 2

    def feature(i, *before):
        mask = lax.dynamic_slice(gate, (role * half, i * count), (half, count)).astype(jnp.float32)
        return (whole_sum(*feat_sums[i], *before) * mask).astype(jnp.bfloat16)

    keep, send = feat_part(feat_size, grads, weight, 0, count, [act_sums[-1][0]])
    first = keep, neighbour(send)
    acts = [activation(0, send)]
    backs = [neighbour(acts[0])]
    keep, send = feat_part(feat_size, grads, weight, count, count, acts)
    second = keep, neighbour(send)
    feat_sums = [across(*pair_sum(*first, send))]
    for i in range(1, len(blocks)):
        acts.append(activation(i, feat_sums[0][0]))
        backs.append(neighbour(acts[i]))
    feat_sums.append(across(*pair_sum(*second, acts[-1])))

    pieces = [piece for pair in zip(acts, backs) for piece in pair]
    kept, middle = halves[0][0].shape[0], layers // 2
    dec_grad = dec_product(grads, pieces, kept, 0, middle, None, [feat_sums[1][0]])
    feat_grads = [feature(0, dec_grad)]
    feat_backs = [neighbour(feat_grads[0])]
    feat_grads.append(feature(1, feat_grads[0]))
    feat_backs.append(neighbour(feat_grads[1]))
    dec_grad = dec_product(grads, pieces, kept, middle, layers - middle, dec_grad, feat_grads[:1])
    enc_grad, bias_grad, feat_grad = enc_product(
        feat_size, blocks, [jnp.concatenate(feat_grads, axis=1)], [jnp.concatenate(feat_backs, axis=1)]
    )
    return (jnp.swapaxes(dec_grad, 1, 2)[None], enc_grad[None], bias_grad, feat_grad[None])


def solution(mesh):
    in_specs = (
        P("layer", "feat", "width"),
        P("layer", "feat", "width"),
        P("layer", "width", "feat"),
        P("layer", "feat"),
        P("layer", None, "feat", "width"),
        P("layer", None, "feat"),
    )
    out_specs = (
        P("layer", None, "feat", "width"),
        P("layer", "width", "feat"),
        P("layer", "feat"),
        P("layer", None, "feat"),
    )
    sizes = (mesh.shape["feat"], mesh.shape["layer"], mesh.shape["width"])
    return jax.shard_map(
        functools.partial(local, *sizes), mesh=mesh, in_specs=in_specs, out_specs=out_specs, check_vma=False
    )
```

```python
import functools

import jax
import jax.numpy as jnp
from jax import lax
from jax.experimental import pallas as pl
from jax.experimental.pallas import tpu as pltpu
from jax.sharding import PartitionSpec as P

MIB = 1 << 20
VMEM = pl.BlockSpec(memory_space=pltpu.VMEM)
ANY = pl.BlockSpec(memory_space=pl.ANY)
HBM = pl.BlockSpec(memory_space=pltpu.HBM)
LIMIT = 16 * MIB
DEC_LIMIT = 24 * MIB
SPLIT = 2


def tile(extent, most):
    best = extent
    for size in range(128, min(extent, most) + 1, 128):
        if extent % size == 0:
            best = size
    return best


def swap(x, axis, size, bit):
    return lax.ppermute(x, axis, [(i, i ^ bit) for i in range(size)])


def cost(rows, depth, columns, passed):
    return pl.CostEstimate(flops=2 * rows * depth * columns, bytes_accessed=passed, transcendentals=0)


def in_hbm(x):
    return pltpu.with_memory_space_constraint(x, pltpu.HBM)


def place_of(feat_size):
    role = lax.rem(lax.axis_index("width"), 2)
    place = lax.axis_index("feat") if feat_size == 2 else 0
    return lax.axis_index("layer"), role ^ place, role


def ordered(low, first, second):
    return jnp.concatenate([jnp.where(low, first, second), jnp.where(low, second, first)], axis=0)


def enc_part_kernel(steps, carried, x_ref, w_hbm, *refs):
    w_ref, x_buf, acc, x_sem, sems = refs[-5:]
    keep_ref, send_ref = refs[carried : carried + 2]
    half = keep_ref.shape[0]
    rows = w_ref.shape[0] // steps

    def get(i):
        here = pl.ds(i * rows, rows)
        return pltpu.make_async_copy(w_hbm.at[here], w_ref.at[here], sems.at[i])

    x_copy = pltpu.make_async_copy(x_ref, x_buf, x_sem)
    x_copy.start()
    if carried:
        carry = pltpu.make_async_copy(refs[0], refs[3], sems.at[steps])
        carry.start()
    for i in range(steps):
        get(i).start()
    x_copy.wait()
    x = ordered(place_of(0)[2] == 0, x_buf[:half], x_buf[half:])
    for i in range(steps):
        get(i).wait()
        here = slice(i * rows, (i + 1) * rows)
        out = jnp.dot(x[:, here], w_ref[here], preferred_element_type=jnp.float32)
        if i:
            out += acc[...]
        if i < steps - 1:
            acc[...] = out
        else:
            keep_ref[...] = out[:half]
            send_ref[...] = out[half:].astype(send_ref.dtype)
    if carried:
        carry.wait()


def enc_part(x, weight, carried=()):
    rows, depth = x.shape
    feats = weight.shape[1]
    half = rows // 2
    steps = next(n for n in (3, 2, 1) if depth % (16 * n) == 0)
    return pl.pallas_call(
        functools.partial(enc_part_kernel, steps, len(carried)),
        in_specs=[ANY, HBM] + [HBM] * len(carried),
        out_specs=[VMEM] * (2 + len(carried)),
        out_shape=[
            jax.ShapeDtypeStruct((half, feats), jnp.float32),
            jax.ShapeDtypeStruct((half, feats), jnp.bfloat16),
        ]
        + [jax.ShapeDtypeStruct(y.shape, y.dtype) for y in carried],
        scratch_shapes=[
            pltpu.VMEM((depth, feats), jnp.bfloat16),
            pltpu.VMEM((rows, depth), jnp.bfloat16),
            pltpu.VMEM((rows, feats), jnp.float32),
            pltpu.SemaphoreType.DMA,
            pltpu.SemaphoreType.DMA((steps + 1,)),
        ],
        compiler_params=pltpu.CompilerParams(vmem_limit_bytes=LIMIT),
        cost_estimate=cost(rows, depth, feats, 2 * depth * feats),
    )(x, in_hbm(weight), *[in_hbm(y) for y in carried])


def feat_part_kernel(feat_size, first, pieces, *refs):
    piece_refs, w_hbm = refs[:pieces], refs[pieces]
    keep_ref, send_ref, w_buf, acc, sems = refs[-5:]
    half, count = keep_ref.shape
    width = count // sems.shape[1]
    source, low, _ = place_of(feat_size)

    def get(k, j):
        return pltpu.make_async_copy(
            w_hbm.at[source ^ k, :, pl.ds(first + j * width, width)],
            w_buf.at[k, :, pl.ds(j * width, width)],
            sems.at[k, j],
        )

    for k in range(pieces):
        for j in range(sems.shape[1]):
            get(k, j).start()
    for k in range(pieces):
        rows = piece_refs[k][...]
        rows = jnp.where((source ^ k) >= source, rows, jnp.zeros_like(rows))
        rows = ordered(low == 0, rows[:half], rows[half:])
        for j in range(sems.shape[1]):
            columns = slice(j * width, (j + 1) * width)
            get(k, j).wait()
            out = jnp.dot(rows, w_buf[k, :, columns], preferred_element_type=jnp.float32)
            if k:
                out += acc[:, columns]
            if k < pieces - 1:
                acc[:, columns] = out
            else:
                keep_ref[:, columns] = out[:half]
                send_ref[:, columns] = out[half:].astype(send_ref.dtype)


def feat_part(feat_size, grads, weight, first, count, after=()):
    tokens, depth = grads[0].shape
    half = tokens // 2
    return pl.pallas_call(
        functools.partial(feat_part_kernel, feat_size, first, len(grads)),
        in_specs=[VMEM] * len(grads) + [HBM] + [ANY] * len(after),
        out_specs=[VMEM, VMEM],
        out_shape=[
            jax.ShapeDtypeStruct((half, count), jnp.float32),
            jax.ShapeDtypeStruct((half, count), jnp.bfloat16),
        ],
        scratch_shapes=[
            pltpu.VMEM((len(grads), depth, count), jnp.bfloat16),
            pltpu.VMEM((tokens, count), jnp.float32),
            pltpu.SemaphoreType.DMA((len(grads), SPLIT if count % (128 * SPLIT) == 0 else 1)),
        ],
        compiler_params=pltpu.CompilerParams(vmem_limit_bytes=LIMIT),
        cost_estimate=cost(tokens, len(grads) * depth, count, 2 * len(grads) * depth * count),
    )(*grads, in_hbm(weight), *after)


def dec_kernel(first_block, blocks, width, kept, grad_refs, act_refs, out_hbm, act_buf, out_buf, sems):
    source, _, role = place_of(0)
    first = role == 0
    steps = act_buf.shape[1] // width

    def gather(columns):
        start = 0
        for mine_ref, other_ref in zip(act_refs[::2], act_refs[1::2]):
            for row in range(0, mine_ref.shape[0], kept):
                mine, other = mine_ref[row : row + kept, columns], other_ref[row : row + kept, columns]
                act_buf[start : start + kept, columns] = jnp.where(first, mine, other)
                act_buf[start + kept : start + 2 * kept, columns] = jnp.where(first, other, mine)
                start += 2 * kept

    def put(b, j):
        columns = pl.ds(j * width, width)
        return pltpu.make_async_copy(
            out_buf.at[b, :, columns], out_hbm.at[source ^ (first_block + b), :, columns], sems.at[b, j]
        )

    for b in range(blocks):
        grad = grad_refs[first_block + b][...]
        grad = jnp.where((source ^ (first_block + b)) >= source, grad, jnp.zeros_like(grad)).T
        for j in range(steps):
            columns = slice(j * width, (j + 1) * width)
            if b == 0:
                gather(columns)
            out = jnp.dot(grad, act_buf[:, columns], preferred_element_type=jnp.float32)
            out_buf[b, :, columns] = out.astype(out_buf.dtype)
            put(b, j).start()
    for b in range(blocks):
        for j in range(steps):
            put(b, j).wait()


def dec_product(grads, acts, kept, first, blocks, before=None, after=()):
    tokens, depth = grads[0].shape
    layers = len(grads)
    feats = acts[0].shape[1]
    held = () if before is None else (before,)
    width = tile(feats, 1024)

    def body(*refs):
        dec_kernel(
            first, blocks, width, kept, refs[:layers], refs[layers : layers + len(acts)], refs[-4], *refs[-3:]
        )

    return pl.pallas_call(
        body,
        in_specs=[VMEM] * (layers + len(acts)) + [ANY] * (len(held) + len(after)),
        out_specs=HBM,
        out_shape=jax.ShapeDtypeStruct((layers, depth, feats), jnp.bfloat16),
        scratch_shapes=[
            pltpu.VMEM((tokens, feats), jnp.bfloat16),
            pltpu.VMEM((blocks, depth, feats), jnp.bfloat16),
            pltpu.SemaphoreType.DMA((blocks, feats // width)),
        ],
        input_output_aliases={layers + len(acts): 0} if held else {},
        compiler_params=pltpu.CompilerParams(vmem_limit_bytes=DEC_LIMIT),
        cost_estimate=cost(blocks * tokens, depth, feats, 2 * blocks * depth * feats),
    )(*grads, *acts, *held, *after)


def enc_kernel(feat_size, width, res_refs, mine_refs, other_refs, outs, res_t, enc_buf, bias_buf, feat_buf, sems):
    enc_hbm, bias_hbm, feat_hbm = outs
    _, low, role = place_of(feat_size)
    low, first = low == 0, role == 0
    res_t[...] = jnp.concatenate([ref[...] for ref in res_refs], axis=0).T
    puts = []

    def put(source, target):
        puts.append(pltpu.make_async_copy(source, target, sems.at[len(puts)]))
        puts[-1].start()

    start = 0
    for mine_ref, other_ref in zip(mine_refs, other_refs):
        count = mine_ref.shape[1]
        here = pl.ds(start, count)
        mine, other = mine_ref[...], other_ref[...]
        feat_buf[:, here] = jnp.concatenate([jnp.where(first, mine, other), jnp.where(first, other, mine)], axis=0)
        put(feat_buf.at[:, here], feat_hbm.at[:, here])
        grad = jnp.concatenate([jnp.where(low, mine, other), jnp.where(low, other, mine)], axis=0)
        for j in range(0, count, width):
            out = jnp.dot(res_t[...], grad[:, j : j + width], preferred_element_type=jnp.float32)
            columns = pl.ds(start + j, width)
            enc_buf[:, columns] = out.astype(enc_buf.dtype)
            put(enc_buf.at[:, columns], enc_hbm.at[:, columns])
        bias_buf[:, here] = jnp.sum(grad.astype(jnp.float32), axis=0, keepdims=True)
        start += count
    put(bias_buf, bias_hbm)
    for copy in puts:
        copy.wait()


def enc_product(feat_size, blocks, mine, others):
    depth = blocks[0].shape[1]
    tokens = 2 * mine[0].shape[0]
    feats = sum(x.shape[1] for x in mine)
    width = tile(mine[0].shape[1], 512)
    ends = [len(blocks), len(blocks) + len(mine), len(blocks) + 2 * len(mine)]

    def body(*refs):
        pieces = refs[: ends[0]], refs[ends[0] : ends[1]], refs[ends[1] : ends[2]]
        enc_kernel(feat_size, width, *pieces, refs[ends[2] : ends[2] + 3], *refs[ends[2] + 3 :])

    return pl.pallas_call(
        body,
        in_specs=[VMEM] * ends[2],
        out_specs=[HBM] * 3,
        out_shape=[
            jax.ShapeDtypeStruct((depth, feats), jnp.bfloat16),
            jax.ShapeDtypeStruct((1, feats), jnp.float32),
            jax.ShapeDtypeStruct((tokens, feats), jnp.bfloat16),
        ],
        scratch_shapes=[
            pltpu.VMEM((depth, tokens), jnp.bfloat16),
            pltpu.VMEM((depth, feats), jnp.bfloat16),
            pltpu.VMEM((1, feats), jnp.float32),
            pltpu.VMEM((tokens, feats), jnp.bfloat16),
            pltpu.SemaphoreType.DMA((1 + len(mine) + feats // width,)),
        ],
        compiler_params=pltpu.CompilerParams(vmem_limit_bytes=LIMIT),
        cost_estimate=cost(tokens, depth, feats, 2 * depth * feats),
    )(*blocks, *mine, *others)


def after(x, *others):
    return lax.optimization_barrier((x, *others))[0] if others else x


def rounded(x):
    return lax.reduce_precision(x, 8, 7)


def local(feat_size, layer_size, width_size, residuals, cotangent, enc_weight, enc_bias, dec_weight, active):
    layers = dec_weight.shape[1]
    source = lax.axis_index("layer")
    role = lax.axis_index("width") % 2
    res, cot = residuals[0], cotangent[0]
    own, depth = res.shape
    feats = enc_weight.shape[2]
    gate = active[0]
    tokens = gate.shape[0]
    weight = jnp.swapaxes(dec_weight[0], 1, 2)

    def neighbour(x):
        return swap(x, "width", width_size, 1)

    def pair_sum(keep, got, *before):
        got = after(got, *before)
        total = rounded(keep + got.astype(jnp.float32))
        return total, total.astype(jnp.bfloat16)

    def across(total, stage):
        bit, parts = 2, []
        while bit < width_size:
            if parts:
                total = rounded(total + parts.pop().astype(jnp.float32))
                stage = total.astype(jnp.bfloat16)
            parts.append(swap(stage, "width", width_size, bit))
            bit *= 2
        return total, parts

    def whole_sum(total, parts, *before):
        for part in parts:
            total = total + after(part, *before).astype(jnp.float32)
        return total

    if feat_size == 2:
        place = lax.axis_index("feat")
        *first_half, cot = enc_part(in_hbm(res), enc_weight[0], [cot])
        halves = [first_half]
        other = after(swap(residuals, "feat", 2, 1), halves[0][1])[0]
        blocks = [res, other]
        starts = [place * own, (1 - place) * own]
        halves.append(enc_part(other, enc_weight[0]))
        grads = jnp.concatenate([cot, after(swap(cot, "feat", 2, 1), halves[1][1])], axis=0)
    else:
        place, halves = 0, []
        blocks = [lax.all_gather(res, "feat", axis=0, tiled=True)]
        starts = [0]
        grads = lax.all_gather(cot, "feat", axis=0, tiled=True)
    for rows in blocks[len(halves) :]:
        halves.append(enc_part(rows, enc_weight[0]))
    sent_back = [neighbour(send) for _, send in halves]
    act_sums = []
    for (keep, _), other in zip(halves, sent_back):
        act_sums.append(across(*pair_sum(keep, other, *[total for total, _ in act_sums[-1:]])))

    held, order = [grads], [0]
    bit = layer_size // 2
    while bit:
        got = after(swap(jnp.stack(held), "layer", layer_size, bit), act_sums[0][0])
        held = held + [got[i] for i in range(len(held))]
        order = order + [o ^ bit for o in order]
        bit //= 2
    grads = [held[order.index(j)] for j in range(layer_size)]

    def activation(i, *before):
        kept = halves[i][0].shape[0]
        mask = lax.dynamic_slice_in_dim(gate, starts[i] + role * kept, kept, 0).astype(jnp.float32)
        return ((whole_sum(*act_sums[i], *before) + enc_bias) * mask).astype(jnp.bfloat16)

    count = feats // 2
    half = tokens // 2

    def feature(i, *before):
        mask = lax.dynamic_slice(gate, (role * half, i * count), (half, count)).astype(jnp.float32)
        return (whole_sum(*feat_sums[i], *before) * mask).astype(jnp.bfloat16)

    keep, send = feat_part(feat_size, grads, weight, 0, count, [act_sums[-1][0]])
    first = keep, neighbour(send)
    acts = [activation(0, send)]
    backs = [neighbour(acts[0])]
    keep, send = feat_part(feat_size, grads, weight, count, count, acts)
    second = keep, neighbour(send)
    feat_sums = [across(*pair_sum(*first, send))]
    for i in range(1, len(blocks)):
        acts.append(activation(i, feat_sums[0][0]))
        backs.append(neighbour(acts[i]))
    feat_sums.append(across(*pair_sum(*second, acts[-1])))

    pieces = [piece for pair in zip(acts, backs) for piece in pair]
    kept, middle = halves[0][0].shape[0], layers // 2
    dec_grad = dec_product(grads, pieces, kept, 0, middle, None, [feat_sums[1][0]])
    feat_grads = [feature(0, dec_grad)]
    feat_backs = [neighbour(feat_grads[0])]
    feat_grads.append(feature(1, feat_grads[0]))
    feat_backs.append(neighbour(feat_grads[1]))
    dec_grad = dec_product(grads, pieces, kept, middle, layers - middle, dec_grad, feat_grads[:1])
    enc_grad, bias_grad, feat_grad = enc_product(
        feat_size, blocks, [jnp.concatenate(feat_grads, axis=1)], [jnp.concatenate(feat_backs, axis=1)]
    )
    return (jnp.swapaxes(dec_grad, 1, 2)[None], enc_grad[None], bias_grad, feat_grad[None])


def solution(mesh):
    in_specs = (
        P("layer", "feat", "width"),
        P("layer", "feat", "width"),
        P("layer", "width", "feat"),
        P("layer", "feat"),
        P("layer", None, "feat", "width"),
        P("layer", None, "feat"),
    )
    out_specs = (
        P("layer", None, "feat", "width"),
        P("layer", "width", "feat"),
        P("layer", "feat"),
        P("layer", None, "feat"),
    )
    sizes = (mesh.shape["feat"], mesh.shape["layer"], mesh.shape["width"])
    return jax.shard_map(
        functools.partial(local, *sizes), mesh=mesh, in_specs=in_specs, out_specs=out_specs, check_vma=False
    )
```

```python
import functools

import jax
import jax.numpy as jnp
from jax import lax
from jax.experimental import pallas as pl
from jax.experimental.pallas import tpu as pltpu
from jax.sharding import PartitionSpec as P

MIB = 1 << 20
VMEM = pl.BlockSpec(memory_space=pltpu.VMEM)
ANY = pl.BlockSpec(memory_space=pl.ANY)
HBM = pl.BlockSpec(memory_space=pltpu.HBM)
LIMIT = 16 * MIB
DEC_LIMIT = 24 * MIB
SPLIT = 2


def tile(extent, most):
    best = extent
    for size in range(128, min(extent, most) + 1, 128):
        if extent % size == 0:
            best = size
    return best


def swap(x, axis, size, bit):
    return lax.ppermute(x, axis, [(i, i ^ bit) for i in range(size)])


def cost(rows, depth, columns, passed):
    return pl.CostEstimate(flops=2 * rows * depth * columns, bytes_accessed=passed, transcendentals=0)


def in_hbm(x):
    return pltpu.with_memory_space_constraint(x, pltpu.HBM)


def place_of(feat_size):
    role = lax.rem(lax.axis_index("width"), 2)
    place = lax.axis_index("feat") if feat_size == 2 else 0
    return lax.axis_index("layer"), role ^ place, role


def ordered(low, first, second):
    return jnp.concatenate([jnp.where(low, first, second), jnp.where(low, second, first)], axis=0)


def enc_part_kernel(steps, carried, x_ref, w_hbm, *refs):
    w_ref, x_buf, acc, x_sem, sems = refs[-5:]
    keep_ref, send_ref = refs[carried : carried + 2]
    half = keep_ref.shape[0]
    rows = w_ref.shape[0] // steps

    def get(i):
        here = pl.ds(i * rows, rows)
        return pltpu.make_async_copy(w_hbm.at[here], w_ref.at[here], sems.at[i])

    x_copy = pltpu.make_async_copy(x_ref, x_buf, x_sem)
    x_copy.start()
    if carried:
        carry = pltpu.make_async_copy(refs[0], refs[3], sems.at[steps])
        carry.start()
    for i in range(steps):
        get(i).start()
    x_copy.wait()
    x = ordered(place_of(0)[2] == 0, x_buf[:half], x_buf[half:])
    for i in range(steps):
        get(i).wait()
        here = slice(i * rows, (i + 1) * rows)
        out = jnp.dot(x[:, here], w_ref[here], preferred_element_type=jnp.float32)
        if i:
            out += acc[...]
        if i < steps - 1:
            acc[...] = out
        else:
            keep_ref[...] = out[:half]
            send_ref[...] = out[half:].astype(send_ref.dtype)
    if carried:
        carry.wait()


def enc_part(x, weight, carried=()):
    rows, depth = x.shape
    feats = weight.shape[1]
    half = rows // 2
    steps = next(n for n in (3, 2, 1) if depth % (16 * n) == 0)
    return pl.pallas_call(
        functools.partial(enc_part_kernel, steps, len(carried)),
        in_specs=[ANY, HBM] + [HBM] * len(carried),
        out_specs=[VMEM] * (2 + len(carried)),
        out_shape=[
            jax.ShapeDtypeStruct((half, feats), jnp.float32),
            jax.ShapeDtypeStruct((half, feats), jnp.bfloat16),
        ]
        + [jax.ShapeDtypeStruct(y.shape, y.dtype) for y in carried],
        scratch_shapes=[
            pltpu.VMEM((depth, feats), jnp.bfloat16),
            pltpu.VMEM((rows, depth), jnp.bfloat16),
            pltpu.VMEM((rows, feats), jnp.float32),
            pltpu.SemaphoreType.DMA,
            pltpu.SemaphoreType.DMA((steps + 1,)),
        ],
        compiler_params=pltpu.CompilerParams(vmem_limit_bytes=LIMIT),
        cost_estimate=cost(rows, depth, feats, 2 * depth * feats),
    )(x, in_hbm(weight), *[in_hbm(y) for y in carried])


def feat_part_kernel(feat_size, first, pieces, *refs):
    piece_refs, w_hbm = refs[:pieces], refs[pieces]
    keep_ref, send_ref, w_buf, acc, sems = refs[-5:]
    half, count = keep_ref.shape
    width = count // sems.shape[1]
    source, low, _ = place_of(feat_size)

    def get(k, j):
        return pltpu.make_async_copy(
            w_hbm.at[source ^ k, :, pl.ds(first + j * width, width)],
            w_buf.at[k, :, pl.ds(j * width, width)],
            sems.at[k, j],
        )

    for k in range(pieces):
        for j in range(sems.shape[1]):
            get(k, j).start()
    for k in range(pieces):
        rows = piece_refs[k][...]
        rows = jnp.where((source ^ k) >= source, rows, jnp.zeros_like(rows))
        rows = ordered(low == 0, rows[:half], rows[half:])
        for j in range(sems.shape[1]):
            columns = slice(j * width, (j + 1) * width)
            get(k, j).wait()
            out = jnp.dot(rows, w_buf[k, :, columns], preferred_element_type=jnp.float32)
            if k:
                out += acc[:, columns]
            if k < pieces - 1:
                acc[:, columns] = out
            else:
                keep_ref[:, columns] = out[:half]
                send_ref[:, columns] = out[half:].astype(send_ref.dtype)


def feat_part(feat_size, grads, weight, first, count, after=()):
    tokens, depth = grads[0].shape
    half = tokens // 2
    return pl.pallas_call(
        functools.partial(feat_part_kernel, feat_size, first, len(grads)),
        in_specs=[VMEM] * len(grads) + [HBM] + [ANY] * len(after),
        out_specs=[VMEM, VMEM],
        out_shape=[
            jax.ShapeDtypeStruct((half, count), jnp.float32),
            jax.ShapeDtypeStruct((half, count), jnp.bfloat16),
        ],
        scratch_shapes=[
            pltpu.VMEM((len(grads), depth, count), jnp.bfloat16),
            pltpu.VMEM((tokens, count), jnp.float32),
            pltpu.SemaphoreType.DMA((len(grads), SPLIT if count % (128 * SPLIT) == 0 else 1)),
        ],
        compiler_params=pltpu.CompilerParams(vmem_limit_bytes=LIMIT),
        cost_estimate=cost(tokens, len(grads) * depth, count, 2 * len(grads) * depth * count),
    )(*grads, in_hbm(weight), *after)


def dec_kernel(first_block, blocks, width, kept, grad_refs, act_refs, out_hbm, act_buf, out_buf, sems):
    source, _, role = place_of(0)
    first = role == 0
    steps = act_buf.shape[1] // width

    def gather(columns):
        start = 0
        for mine_ref, other_ref in zip(act_refs[::2], act_refs[1::2]):
            for row in range(0, mine_ref.shape[0], kept):
                mine, other = mine_ref[row : row + kept, columns], other_ref[row : row + kept, columns]
                act_buf[start : start + kept, columns] = jnp.where(first, mine, other)
                act_buf[start + kept : start + 2 * kept, columns] = jnp.where(first, other, mine)
                start += 2 * kept

    def put(b, j):
        columns = pl.ds(j * width, width)
        return pltpu.make_async_copy(
            out_buf.at[b, :, columns], out_hbm.at[source ^ (first_block + b), :, columns], sems.at[b, j]
        )

    for b in range(blocks):
        grad = grad_refs[first_block + b][...]
        grad = jnp.where((source ^ (first_block + b)) >= source, grad, jnp.zeros_like(grad)).T
        for j in range(steps):
            columns = slice(j * width, (j + 1) * width)
            if b == 0:
                gather(columns)
            out = jnp.dot(grad, act_buf[:, columns], preferred_element_type=jnp.float32)
            out_buf[b, :, columns] = out.astype(out_buf.dtype)
            put(b, j).start()
    for b in range(blocks):
        for j in range(steps):
            put(b, j).wait()


def dec_product(grads, acts, kept, first, blocks, before=None, after=()):
    tokens, depth = grads[0].shape
    layers = len(grads)
    feats = acts[0].shape[1]
    held = () if before is None else (before,)
    width = tile(feats, 1024)

    def body(*refs):
        dec_kernel(
            first, blocks, width, kept, refs[:layers], refs[layers : layers + len(acts)], refs[-4], *refs[-3:]
        )

    return pl.pallas_call(
        body,
        in_specs=[VMEM] * (layers + len(acts)) + [ANY] * (len(held) + len(after)),
        out_specs=HBM,
        out_shape=jax.ShapeDtypeStruct((layers, depth, feats), jnp.bfloat16),
        scratch_shapes=[
            pltpu.VMEM((tokens, feats), jnp.bfloat16),
            pltpu.VMEM((blocks, depth, feats), jnp.bfloat16),
            pltpu.SemaphoreType.DMA((blocks, feats // width)),
        ],
        input_output_aliases={layers + len(acts): 0} if held else {},
        compiler_params=pltpu.CompilerParams(vmem_limit_bytes=DEC_LIMIT),
        cost_estimate=cost(blocks * tokens, depth, feats, 2 * blocks * depth * feats),
    )(*grads, *acts, *held, *after)


def enc_kernel(feat_size, width, res_refs, mine_refs, other_refs, outs, res_t, enc_buf, bias_buf, feat_buf, sems):
    enc_hbm, bias_hbm, feat_hbm = outs
    _, low, role = place_of(feat_size)
    low, first = low == 0, role == 0
    res_t[...] = jnp.concatenate([ref[...] for ref in res_refs], axis=0).T
    puts = []

    def put(source, target):
        puts.append(pltpu.make_async_copy(source, target, sems.at[len(puts)]))
        puts[-1].start()

    start = 0
    for mine_ref, other_ref in zip(mine_refs, other_refs):
        count = mine_ref.shape[1]
        here = pl.ds(start, count)
        mine, other = mine_ref[...], other_ref[...]
        feat_buf[:, here] = jnp.concatenate([jnp.where(first, mine, other), jnp.where(first, other, mine)], axis=0)
        put(feat_buf.at[:, here], feat_hbm.at[:, here])
        grad = jnp.concatenate([jnp.where(low, mine, other), jnp.where(low, other, mine)], axis=0)
        for j in range(0, count, width):
            out = jnp.dot(res_t[...], grad[:, j : j + width], preferred_element_type=jnp.float32)
            columns = pl.ds(start + j, width)
            enc_buf[:, columns] = out.astype(enc_buf.dtype)
            put(enc_buf.at[:, columns], enc_hbm.at[:, columns])
        bias_buf[:, here] = jnp.sum(grad.astype(jnp.float32), axis=0, keepdims=True)
        start += count
    put(bias_buf, bias_hbm)
    for copy in puts:
        copy.wait()


def enc_product(feat_size, blocks, mine, others):
    depth = blocks[0].shape[1]
    tokens = 2 * mine[0].shape[0]
    feats = sum(x.shape[1] for x in mine)
    width = tile(mine[0].shape[1], 512)
    ends = [len(blocks), len(blocks) + len(mine), len(blocks) + 2 * len(mine)]

    def body(*refs):
        pieces = refs[: ends[0]], refs[ends[0] : ends[1]], refs[ends[1] : ends[2]]
        enc_kernel(feat_size, width, *pieces, refs[ends[2] : ends[2] + 3], *refs[ends[2] + 3 :])

    return pl.pallas_call(
        body,
        in_specs=[VMEM] * ends[2],
        out_specs=[HBM] * 3,
        out_shape=[
            jax.ShapeDtypeStruct((depth, feats), jnp.bfloat16),
            jax.ShapeDtypeStruct((1, feats), jnp.float32),
            jax.ShapeDtypeStruct((tokens, feats), jnp.bfloat16),
        ],
        scratch_shapes=[
            pltpu.VMEM((depth, tokens), jnp.bfloat16),
            pltpu.VMEM((depth, feats), jnp.bfloat16),
            pltpu.VMEM((1, feats), jnp.float32),
            pltpu.VMEM((tokens, feats), jnp.bfloat16),
            pltpu.SemaphoreType.DMA((1 + len(mine) + feats // width,)),
        ],
        compiler_params=pltpu.CompilerParams(vmem_limit_bytes=LIMIT),
        cost_estimate=cost(tokens, depth, feats, 2 * depth * feats),
    )(*blocks, *mine, *others)


def after(x, *others):
    return lax.optimization_barrier((x, *others))[0] if others else x


def rounded(x):
    return lax.reduce_precision(x, 8, 7)


def local(feat_size, layer_size, width_size, residuals, cotangent, enc_weight, enc_bias, dec_weight, active):
    layers = dec_weight.shape[1]
    source = lax.axis_index("layer")
    role = lax.axis_index("width") % 2
    res, cot = residuals[0], cotangent[0]
    own, depth = res.shape
    feats = enc_weight.shape[2]
    gate = active[0]
    tokens = gate.shape[0]
    weight = jnp.swapaxes(dec_weight[0], 1, 2)

    def neighbour(x):
        return swap(x, "width", width_size, 1)

    def pair_sum(keep, got, *before):
        got = after(got, *before)
        total = rounded(keep + got.astype(jnp.float32))
        return total, total.astype(jnp.bfloat16)

    def across(total, stage):
        bit, parts = 2, []
        while bit < width_size:
            if parts:
                total = rounded(total + parts.pop().astype(jnp.float32))
                stage = total.astype(jnp.bfloat16)
            parts.append(swap(stage, "width", width_size, bit))
            bit *= 2
        return total, parts

    def whole_sum(total, parts, *before):
        for part in parts:
            total = total + after(part, *before).astype(jnp.float32)
        return total

    if feat_size == 2:
        place = lax.axis_index("feat")
        *first_half, cot = enc_part(in_hbm(res), enc_weight[0], [cot])
        halves = [first_half]
        other = after(swap(residuals, "feat", 2, 1), halves[0][1])[0]
        blocks = [res, other]
        starts = [place * own, (1 - place) * own]
        halves.append(enc_part(other, enc_weight[0]))
        grads = jnp.concatenate([cot, after(swap(cot, "feat", 2, 1), halves[1][1])], axis=0)
    else:
        place, halves = 0, []
        blocks = [lax.all_gather(res, "feat", axis=0, tiled=True)]
        starts = [0]
        grads = lax.all_gather(cot, "feat", axis=0, tiled=True)
    for rows in blocks[len(halves) :]:
        halves.append(enc_part(rows, enc_weight[0]))
    sent_back = [neighbour(send) for _, send in halves]
    act_sums = []
    for (keep, _), other in zip(halves, sent_back):
        act_sums.append(across(*pair_sum(keep, other, *[total for total, _ in act_sums[-1:]])))

    held, order = [grads], [0]
    bit = layer_size // 2
    while bit:
        got = after(swap(jnp.stack(held), "layer", layer_size, bit), act_sums[0][0])
        held = held + [got[i] for i in range(len(held))]
        order = order + [o ^ bit for o in order]
        bit //= 2
    grads = [held[order.index(j)] for j in range(layer_size)]

    def activation(i, *before):
        kept = halves[i][0].shape[0]
        mask = lax.dynamic_slice_in_dim(gate, starts[i] + role * kept, kept, 0).astype(jnp.float32)
        return ((whole_sum(*act_sums[i], *before) + enc_bias) * mask).astype(jnp.bfloat16)

    count = feats // 2
    half = tokens // 2

    def feature(i, *before):
        mask = lax.dynamic_slice(gate, (role * half, i * count), (half, count)).astype(jnp.float32)
        return (whole_sum(*feat_sums[i], *before) * mask).astype(jnp.bfloat16)

    keep, send = feat_part(feat_size, grads, weight, 0, count, [act_sums[-1][0]])
    first = keep, neighbour(send)
    acts = [activation(0, keep)]
    backs = [neighbour(acts[0])]
    keep, send = feat_part(feat_size, grads, weight, count, count, acts)
    second = keep, neighbour(send)
    feat_sums = [across(*pair_sum(*first, keep))]
    for i in range(1, len(blocks)):
        acts.append(activation(i, feat_sums[0][0]))
        backs.append(neighbour(acts[i]))
    feat_sums.append(across(*pair_sum(*second, feat_sums[0][0])))

    pieces = [piece for pair in zip(acts, backs) for piece in pair]
    kept, middle = halves[0][0].shape[0], layers // 2
    dec_grad = dec_product(grads, pieces, kept, 0, middle, None, [feat_sums[1][0]])
    feat_grads = [feature(0, dec_grad)]
    feat_backs = [neighbour(feat_grads[0])]
    feat_grads.append(feature(1, feat_grads[0]))
    feat_backs.append(neighbour(feat_grads[1]))
    dec_grad = dec_product(grads, pieces, kept, middle, layers - middle, dec_grad, feat_grads[:1])
    enc_grad, bias_grad, feat_grad = enc_product(
        feat_size, blocks, [jnp.concatenate(feat_grads, axis=1)], [jnp.concatenate(feat_backs, axis=1)]
    )
    return (jnp.swapaxes(dec_grad, 1, 2)[None], enc_grad[None], bias_grad, feat_grad[None])


def solution(mesh):
    in_specs = (
        P("layer", "feat", "width"),
        P("layer", "feat", "width"),
        P("layer", "width", "feat"),
        P("layer", "feat"),
        P("layer", None, "feat", "width"),
        P("layer", None, "feat"),
    )
    out_specs = (
        P("layer", None, "feat", "width"),
        P("layer", "width", "feat"),
        P("layer", "feat"),
        P("layer", None, "feat"),
    )
    sizes = (mesh.shape["feat"], mesh.shape["layer"], mesh.shape["width"])
    return jax.shard_map(
        functools.partial(local, *sizes), mesh=mesh, in_specs=in_specs, out_specs=out_specs, check_vma=False
    )
```
